32 devices in a mesh: sig: 16 (over z, y, x), xf: 2 (over core).
Axes of the slice: x: 2, y: 2, z: 4, core: 2. Of those that a mesh axis runs over, the one named last changes fastest.
Arguments:
- coef: bfloat16 [256, 512], P('sig', 'xf'), may hold values from -6 to 6
- sym_alpha: int32 [256], P('sig'), may hold values from 0 to 1
- sym_beta: int32 [512], P('xf'), may hold values from 0 to 1
- win_target: int32 [256, 16], P('sig'), may hold values from 0 to 255
- win_pair: int32 [256, 16], P('sig'), may hold values from 0 to 31
- win_flip: int32 [256, 16], P('sig'), may hold values from 0 to 1
- rep_target: int32 [256, 512], P('sig'), may hold values from 0 to 255
- rep_pair: int32 [256, 512], P('sig'), may hold values from 0 to 4095
- rep_flip: int32 [256, 512], P('sig'), may hold values from 0 to 1
- half_ints: bfloat16 [32, 16384], P('xf'), may hold values from -0.06591797 to 0.06591797
- orbitals: bfloat16 [128, 64], replicated, may hold values from -0.5 to 0.5
- orb_sym: int32 [64], replicated, may hold values from 0 to 1
- pair_sym: int32 [32], P('xf'), may hold values from 0 to 1
Outputs:
- sigma: float32 [256, 512], P('sig', 'xf')
The draws below stay inside these ranges and needn't reach their ends.
All inputs are finite; a program needn't handle non-finite values.
Results may differ from the reference program's by a relative error of at most 0.0041.
Values may be sent and summed in bfloat16 or wider, within the bound.
A program may use at most 64 MiB of HBM per device.

```python
import jax
import jax.numpy as jnp
from jax import lax

NORB = 64
NBAS = 128
WREP = 16
NREP = 512
NA = 256
NB = 512
KW = 32
NPAIR = 4096


def place_ends(entries, own_key, least, high):
    longest = entries.shape.index(max(entries.shape))
    spots = []
    for shift in (0, 1):
        where = [jax.random.randint(jax.random.fold_in(own_key, axis), (), 0, length) for axis, length in enumerate(entries.shape)]
        where[longest] = (where[longest] + shift) % entries.shape[longest]
        spots.append(tuple(where))
    return entries.at[spots[0]].set(least).at[spots[1]].set(high)


def block_levels(stream_key, extent, shards, smallest, largest):
    factor_of, own = 1.0, jax.random.fold_in(stream_key, 6)
    for position, shards_of in shards:
        draws = jnp.exp(jax.random.uniform(jax.random.fold_in(own, position), (shards_of,), jnp.float32, smallest / len(shards), largest / len(shards)))
        factor_of = factor_of * jnp.repeat(draws, extent[position] // shards_of).reshape([-1 if axis == position else 1 for axis in range(len(extent))])
    return factor_of


def centred(key, dims, scale, reach, cuts=(), kind=jnp.bfloat16):
    array = scale * jax.random.normal(key, dims, jnp.float32)
    if cuts:
        array = array * block_levels(key, dims, cuts, -0.22, 0.18)
    return jnp.clip(array, -reach, reach).astype(kind)


def setup_inputs(seed: int = 0) -> dict:
    splits = jax.random.split(jax.random.key(seed), 14)
    return {
        "coef": centred(splits[0], (NA, NB), 1.0, 6.0, ((0, 16), (1, 2))),
        "sym_alpha": place_ends(jax.random.randint(splits[1], (NA,), 0, 2), jax.random.fold_in(splits[1], 1), 0, 1).astype(jnp.int32),
        "sym_beta": place_ends(jax.random.randint(splits[2], (NB,), 0, 2), jax.random.fold_in(splits[2], 1), 0, 1).astype(jnp.int32),
        "win_target": place_ends(jax.random.randint(splits[3], (NA, WREP), 0, NA), jax.random.fold_in(splits[3], 1), 0, NA - 1).astype(jnp.int32),
        "win_pair": place_ends(jax.random.randint(splits[4], (NA, WREP), 0, KW), jax.random.fold_in(splits[4], 1), 0, KW - 1).astype(jnp.int32),
        "win_flip": place_ends(jax.random.randint(splits[5], (NA, WREP), 0, 2), jax.random.fold_in(splits[5], 1), 0, 1).astype(jnp.int32),
        "rep_target": place_ends(jax.random.randint(splits[6], (NA, NREP), 0, NA), jax.random.fold_in(splits[6], 1), 0, NA - 1).astype(jnp.int32),
        "rep_pair": place_ends(jax.random.randint(splits[7], (NA, NREP), 0, NPAIR), jax.random.fold_in(splits[7], 1), 0, NPAIR - 1).astype(jnp.int32),
        "rep_flip": place_ends(jax.random.randint(splits[8], (NA, NREP), 0, 2), jax.random.fold_in(splits[8], 1), 0, 1).astype(jnp.int32),
        "half_ints": centred(splits[9], (KW, NBAS * NBAS), 0.011, 0.06591797, ((0, 2),)),
        "orbitals": centred(splits[10], (NBAS, NORB), NBAS ** -0.5, 0.5),
        "orb_sym": place_ends(jax.random.randint(splits[11], (NORB,), 0, 2), jax.random.fold_in(splits[11], 1), 0, 1).astype(jnp.int32),
        "pair_sym": place_ends(jax.random.randint(splits[12], (KW,), 0, 2), jax.random.fold_in(splits[12], 1), 0, 1).astype(jnp.int32),
    }


def transform(half_ints, orbitals, orb_sym, pair_sym):
    rows = half_ints.shape[0]
    cube = half_ints.reshape(rows, NBAS, NBAS).astype(jnp.float32)
    first = jnp.einsum('mpq,qj->mpj', cube, orbitals.astype(jnp.float32)).astype(jnp.bfloat16)
    first = lax.optimization_barrier(first)
    full = jnp.einsum('pi,mpj->mij', orbitals.astype(jnp.float32), first.astype(jnp.float32))
    parity = jnp.bitwise_xor(orb_sym[:, None], orb_sym[None, :])
    keep = parity[None, :, :] == pair_sym[:, None, None]
    return jnp.where(keep, full, 0.0).astype(jnp.bfloat16).reshape(rows, NORB * NORB)


def reference(coef, sym_alpha, sym_beta, win_target, win_pair, win_flip, rep_target, rep_pair, rep_flip, half_ints, orbitals, orb_sym, pair_sym):
    allowed = jnp.bitwise_xor(sym_alpha[:, None], sym_beta[None, :]) == 0
    c_eff = jnp.where(allowed, coef, jnp.zeros_like(coef)).astype(jnp.bfloat16)
    ints = transform(half_ints, orbitals, orb_sym, pair_sym)
    columns = jnp.arange(KW, dtype=jnp.int32)

    def step(terms, inputs):
        w_tgt, w_pair, w_flip, r_tgt, r_pair, r_flip = inputs
        rows = c_eff[w_tgt]
        picks = ((w_pair[:, None] == columns[None, :]) * (1 - 2 * w_flip)[:, None]).astype(jnp.bfloat16)
        dens = lax.dot_general(rows, picks, (((0,), (0,)), ((), ())), preferred_element_type=jnp.float32).astype(jnp.bfloat16)
        inter = jnp.dot(dens, ints, preferred_element_type=jnp.float32)
        chosen = jnp.take(inter, r_pair, axis=1) * (1 - 2 * r_flip).astype(jnp.float32)[None, :]
        return terms.at[r_tgt].add(chosen.T), None

    start = jnp.zeros((NA, NB), jnp.float32)
    terms = lax.scan(step, start, (win_target, win_pair, win_flip, rep_target, rep_pair, rep_flip))[0]
    return jnp.where(allowed, terms, jnp.zeros_like(terms))
```

```python
import functools

import jax
import jax.numpy as jnp
from jax import lax
from jax.experimental import pallas as pl
from jax.experimental.pallas import tpu as pltpu
from jax.sharding import PartitionSpec as P

MESH = pl.DeviceIdType.MESH
NT = (((1,), (1,)), ((), ()))
TN = (((0,), (0,)), ((), ()))
NN = (((1,), (0,)), ((), ()))
F32 = jnp.float32
BF16 = jnp.bfloat16
LANES = 128


def dot(x, y, dims):
    return lax.dot_general(x, y, dims, preferred_element_type=F32)


def split(x):
    high = x.astype(BF16)
    return high, (x - high.astype(F32)).astype(BF16)


def for_each(count, step):
    if count <= 2:
        for index in range(count):
            step(index)
    else:
        lax.fori_loop(0, count, lambda index, _: (step(index), 0)[1], 0)


def column(row, count):
    n = row.shape[1]
    mine = lax.broadcasted_iota(jnp.int32, (count, n), 0)
    other = lax.broadcasted_iota(jnp.int32, (count, n), 1)
    return jnp.sum(jnp.where(mine == other, row, 0), axis=1, keepdims=True)


def transform(half_ref, orb_ref, orb_sym_ref, pair_sym_ref, first_ref, block_ref, table_ref):
    rows = half_ref.shape[0]
    n_bas, n_orb = orb_ref.shape
    half = n_orb * n_orb // LANES
    orb = orb_ref[...]
    twice = jnp.concatenate([orb, orb], axis=1)
    group = 16

    def first_step(c):
        base = c * group * n_bas
        parts = [half_ref[:, pl.ds(pl.multiple_of(base + k * n_bas, LANES), n_bas)] for k in range(group)]
        first = dot(jnp.concatenate(parts, axis=0), twice, NN)
        start = pl.multiple_of(c * (group * rows), group * rows)
        first_ref[pl.ds(start, group * rows), :] = first.astype(BF16).astype(F32)

    for c in range(n_bas // group):
        first_step(c)

    lane = lax.broadcasted_iota(jnp.int32, (half, LANES), 1)
    low = lane < n_orb
    sym = orb_sym_ref[...].reshape(1, n_orb)
    sym_i = column(sym, n_orb)
    parity = jnp.bitwise_xor(
        jnp.where(low, sym_i[:half], sym_i[half:]), jnp.concatenate([sym, sym], axis=1)
    )
    orb_t = orb.astype(F32).T.astype(BF16)
    for m in range(rows):
        part = first_ref[pl.ds(m, n_bas, stride=rows), :].astype(BF16)
        full = dot(orb_t, part, NN)
        full = jnp.where(low, full[:half], full[half:])
        full = jnp.where(parity == pair_sym_ref[m], full, 0.0)
        block_ref[m * half : (m + 1) * half, :] = full.astype(BF16).astype(F32)
    for h in range(half):
        table_ref[h * rows : (h + 1) * rows, :] = block_ref[pl.ds(h, rows, stride=half), :]


def couple(a, own, n_orb, win, rep, table_ref, g_ref, w_ref):
    win_target_ref, win_pair_ref, win_flip_ref = win
    rep_target_ref, rep_pair_ref, rep_flip_ref = rep
    half = n_orb * n_orb // LANES
    rows = table_ref.shape[0] // half
    n_all = g_ref.shape[1]
    n_rep = rep_pair_ref.shape[1]
    row = pl.ds(a, 1)
    pair = rep_pair_ref[row, :]
    orb_i = pair // n_orb
    orb_j = pair % n_orb
    place = (orb_i // half) * n_orb + orb_j
    which = orb_i % half
    blocks = n_rep // LANES
    places = [jnp.broadcast_to(place[:, k * LANES : (k + 1) * LANES], (8, LANES)) for k in range(blocks)]
    whiches = [jnp.broadcast_to(which[:, k * LANES : (k + 1) * LANES], (8, LANES)) for k in range(blocks)]
    picked = [[jnp.zeros((8, LANES), F32) for _ in range(rows // 8)] for _ in range(blocks)]
    for h in range(half):
        hits = [whiches[k] == h for k in range(blocks)]
        for s in range(rows // 8):
            table = table_ref[h * rows + s * 8 : h * rows + (s + 1) * 8, :]
            for k in range(blocks):
                got = jnp.take_along_axis(table, places[k], axis=1, mode="promise_in_bounds")
                picked[k][s] = jnp.where(hits[k], got, picked[k][s])
    chosen = jnp.concatenate([jnp.concatenate(p, axis=0) for p in picked], axis=1)
    sign = (1 - 2 * rep_flip_ref[row, :]).astype(F32)
    chosen = (chosen * sign).astype(BF16)
    target = rep_target_ref[row, :]
    w_target = win_target_ref[row, :]
    w_pair = win_pair_ref[row, :]
    w_sign = (1 - 2 * win_flip_ref[row, :]).astype(F32)
    n_win = w_pair.shape[1]
    m_own = lax.broadcasted_iota(jnp.int32, (rows, n_win), 0) + own * rows
    picks = jnp.where(m_own == w_pair, w_sign, 0.0).astype(BF16)
    store = pl.ds(pl.multiple_of(a * rows, rows), rows)
    tile = 256

    def strings(k):
        base = k * tile
        t = lax.broadcasted_iota(jnp.int32, (tile, n_rep), 0) + base
        hit = jnp.where(t == target, 1.0, 0.0).astype(BF16)
        s = lax.broadcasted_iota(jnp.int32, (tile, n_win), 0) + base
        reach = jnp.where(s == w_target, 1.0, 0.0).astype(BF16)
        cols = pl.ds(pl.multiple_of(base, tile), tile)
        g_ref[store, cols] = dot(chosen, hit, NT)
        w_ref[store, cols] = dot(picks, reach, NT)

    for_each(n_all // tile, strings)


def kernel(
    n_sig, n_xf,
    coef_ref, sym_alpha_ref, sym_beta_ref,
    win_target_ref, win_pair_ref, win_flip_ref,
    rep_target_ref, rep_pair_ref, rep_flip_ref,
    half_ref, orb_ref, orb_sym_ref, pair_sym_ref,
    out_ref,
    first_ref, block_ref, table_ref, g_ref, w_ref,
    c_ref, q_ref, q_in, p_ref, p_in, h_ref,
    c_send, c_recv, q_send, q_recv, p_send, p_recv, h_send, h_recv,
):
    me = lax.axis_index("sig")
    own = lax.axis_index("xf")
    own_rows, n_beta = coef_ref.shape
    n_orb = orb_ref.shape[1]
    n_all = own_rows * n_sig
    width = n_all // n_xf

    barrier = pltpu.get_barrier_semaphore()

    def greet_sig(k):
        pl.semaphore_signal(barrier, inc=1, device_id=(lax.rem(me + k, n_sig), own), device_id_type=MESH)

    def greet_xf(k):
        pl.semaphore_signal(barrier, inc=1, device_id=(me, lax.rem(own + k, n_xf)), device_id_type=MESH)

    for k in range(1, n_sig):
        greet_sig(k)
    for k in range(1, n_xf):
        greet_xf(k)

    sym_alpha = column(sym_alpha_ref[...].reshape(1, own_rows), own_rows)
    sym_beta = sym_beta_ref[...].reshape(1, n_beta)
    allowed = jnp.bitwise_xor(sym_alpha, sym_beta) == 0
    c_ref[me] = jnp.where(allowed, coef_ref[...].astype(F32), 0.0).astype(BF16)

    transform(half_ref, orb_ref, orb_sym_ref, pair_sym_ref, first_ref, block_ref, table_ref)

    pl.semaphore_wait(barrier, n_sig + n_xf - 2)

    def c_copy(k):
        return pltpu.make_async_remote_copy(
            src_ref=c_ref.at[me], dst_ref=c_ref.at[me], send_sem=c_send.at[k], recv_sem=c_recv.at[k],
            device_id=(lax.rem(me + k, n_sig), own), device_id_type=MESH)

    def c_arrival(k):
        slot = lax.rem(me + n_sig - k, n_sig)
        return pltpu.make_async_remote_copy(
            src_ref=c_ref.at[slot], dst_ref=c_ref.at[slot], send_sem=c_send.at[k], recv_sem=c_recv.at[k],
            device_id=(lax.rem(me + k, n_sig), own), device_id_type=MESH)

    def loop(low, high, step):
        lax.fori_loop(low, high, lambda k, _: (step(k), 0)[1], 0)

    loop(1, n_sig, lambda k: c_copy(k).start())

    win = (win_target_ref, win_pair_ref, win_flip_ref)
    rep = (rep_target_ref, rep_pair_ref, rep_flip_ref)
    loop(0, own_rows, lambda a: couple(a, own, n_orb, win, rep, table_ref, g_ref, w_ref))

    depth = g_ref.shape[0]
    tile = 256

    def q_tile(t, x):
        cols = pl.ds(pl.multiple_of(t * tile, tile), tile)
        lanes = pl.ds(pl.multiple_of(x * width, width), width)
        if depth == tile:
            high, low = split(g_ref[:, cols])
            w = w_ref[:, lanes].astype(BF16)
            total = dot(high, w, TN) + dot(low, w, TN)
        else:
            def part(k, total):
                ks = pl.ds(pl.multiple_of(k * tile, tile), tile)
                high, low = split(g_ref[ks, cols])
                w = w_ref[ks, lanes].astype(BF16)
                return total + dot(high, w, TN) + dot(low, w, TN)
            total = lax.fori_loop(0, depth // tile, part, jnp.zeros((tile, width), F32))
        q_ref[x, cols, :] = total

    for_each(n_xf, lambda x: for_each(n_all // tile, lambda t: q_tile(t, x)))

    def q_copy(k):
        there = lax.rem(own + k, n_xf)
        return pltpu.make_async_remote_copy(
            src_ref=q_ref.at[there], dst_ref=q_in.at[k - 1], send_sem=q_send.at[k - 1], recv_sem=q_recv.at[k - 1],
            device_id=(me, there), device_id_type=MESH)

    for k in range(1, n_xf):
        q_copy(k).start()
    for k in range(1, n_xf):
        q_copy(k).wait_recv()

    def p_block(t):
        rows = pl.ds(pl.multiple_of(t * tile, tile), tile)
        total = q_ref[own, rows, :]
        for k in range(n_xf - 1):
            total = total + q_in[k, rows, :]
        per = tile // own_rows
        p_ref[pl.ds(t * per, per)] = total.astype(BF16).reshape(per, own_rows, width)

    for_each(n_all // tile, p_block)

    def p_copy(k):
        there = lax.rem(me + k, n_sig)
        return pltpu.make_async_remote_copy(
            src_ref=p_ref.at[there], dst_ref=p_in.at[k], send_sem=p_send.at[k], recv_sem=p_recv.at[k],
            device_id=(there, own), device_id_type=MESH)

    loop(1, n_sig, lambda k: p_copy(k).start())
    p_in[0] = p_ref[me]
    loop(1, n_sig, lambda k: p_copy(k).wait_recv())
    h_ref[own] = jnp.sum(p_in[...].astype(F32), axis=0)

    def h_copy(k):
        return pltpu.make_async_remote_copy(
            src_ref=h_ref.at[own], dst_ref=h_ref.at[own], send_sem=h_send.at[k - 1], recv_sem=h_recv.at[k - 1],
            device_id=(me, lax.rem(own + k, n_xf)), device_id_type=MESH)

    def h_arrival(k):
        slot = lax.rem(own + n_xf - k, n_xf)
        return pltpu.make_async_remote_copy(
            src_ref=h_ref.at[slot], dst_ref=h_ref.at[slot], send_sem=h_send.at[k - 1], recv_sem=h_recv.at[k - 1],
            device_id=(me, lax.rem(own + k, n_xf)), device_id_type=MESH)

    for k in range(1, n_xf):
        h_copy(k).start()
    loop(1, n_sig, lambda k: c_arrival(k).wait_recv())
    for k in range(1, n_xf):
        h_arrival(k).wait_recv()
    high, low = split(jnp.concatenate([h_ref[x] for x in range(n_xf)], axis=1))
    c_all = c_ref[...].reshape(n_all, n_beta)
    total = dot(high, c_all, NN) + dot(low, c_all, NN)
    out_ref[...] = jnp.where(allowed, total, 0.0)

    loop(1, n_sig, lambda k: c_copy(k).wait_send())
    loop(1, n_sig, lambda k: p_copy(k).wait_send())
    for k in range(1, n_xf):
        q_copy(k).wait_send()
        h_copy(k).wait_send()


def body(n_sig, n_xf, *args):
    coef, half_ints, orbitals = args[0], args[9], args[10]
    own_rows, n_beta = coef.shape
    rows = half_ints.shape[0]
    n_bas, n_orb = orbitals.shape
    n_all = own_rows * n_sig
    width = n_all // n_xf
    half = n_orb * n_orb // LANES
    vmem = pl.BlockSpec(memory_space=pltpu.VMEM)
    smem = pl.BlockSpec(memory_space=pltpu.SMEM)
    dma = pltpu.SemaphoreType.DMA
    return pl.pallas_call(
        functools.partial(kernel, n_sig, n_xf),
        out_shape=jax.ShapeDtypeStruct((own_rows, n_beta), F32),
        in_specs=[vmem] * 12 + [smem],
        out_specs=vmem,
        scratch_shapes=[
            pltpu.VMEM((n_bas * rows, LANES), F32),
            pltpu.VMEM((rows * half, LANES), F32),
            pltpu.VMEM((rows * half, LANES), F32),
            pltpu.VMEM((own_rows * rows, n_all), F32),
            pltpu.VMEM((own_rows * rows, n_all), F32),
            pltpu.VMEM((n_sig, own_rows, n_beta), BF16),
            pltpu.VMEM((n_xf, n_all, width), F32),
            pltpu.VMEM((n_xf - 1, n_all, width), F32),
            pltpu.VMEM((n_sig, own_rows, width), BF16),
            pltpu.VMEM((n_sig, own_rows, width), BF16),
            pltpu.VMEM((n_xf, own_rows, width), F32),
            dma((n_sig,)), dma((n_sig,)),
            dma((n_xf - 1,)), dma((n_xf - 1,)),
            dma((n_sig,)), dma((n_sig,)),
            dma((n_xf - 1,)), dma((n_xf - 1,)),
        ],
        compiler_params=pltpu.CompilerParams(
            collective_id=0, has_side_effects=True, vmem_limit_bytes=40 * 1024 * 1024
        ),
    )(*args)


def solution(mesh):
    in_specs = (
        P("sig", "xf"), P("sig"), P("xf"),
        P("sig", None), P("sig", None), P("sig", None),
        P("sig", None), P("sig", None), P("sig", None),
        P("xf", None), P(), P(), P("xf"),
    )
    step = functools.partial(body, mesh.shape["sig"], mesh.shape["xf"])
    return jax.shard_map(step, mesh=mesh, in_specs=in_specs, out_specs=P("sig", "xf"), check_vma=False)
```

```python
import functools

import jax
import jax.numpy as jnp
from jax import lax
from jax.experimental import pallas as pl
from jax.experimental.pallas import tpu as pltpu
from jax.sharding import PartitionSpec as P

MESH = pl.DeviceIdType.MESH
NT = (((1,), (1,)), ((), ()))
TN = (((0,), (0,)), ((), ()))
NN = (((1,), (0,)), ((), ()))
F32 = jnp.float32
BF16 = jnp.bfloat16
LANES = 128
WIDE = 256


def dot(x, y, dims):
    return lax.dot_general(x, y, dims, preferred_element_type=F32)


def split(x):
    high = x.astype(BF16)
    return high, (x - high.astype(F32)).astype(BF16)


def for_each(count, step):
    if count <= 2:
        for index in range(count):
            step(index)
    else:
        lax.fori_loop(0, count, lambda index, _: (step(index), 0)[1], 0)


def column(row, count):
    n = row.shape[1]
    mine = lax.broadcasted_iota(jnp.int32, (count, n), 0)
    other = lax.broadcasted_iota(jnp.int32, (count, n), 1)
    return jnp.sum(jnp.where(mine == other, row, 0), axis=1, keepdims=True)


def transform(half_ref, orb_ref, orb_sym_ref, pair_sym_ref, first_ref, block_ref, table_ref):
    rows = half_ref.shape[0]
    n_orb, n_bas = orb_ref.shape
    orb_t = orb_ref[...]
    twice = jnp.concatenate([orb_t, orb_t], axis=0)
    group = 16

    for c in range(n_bas // group):
        base = c * group * n_bas
        parts = [half_ref[:, base + k * n_bas : base + (k + 1) * n_bas] for k in range(group)]
        first = dot(jnp.concatenate(parts, axis=0), twice, NT)
        start = c * (group * rows)
        first_ref[start : start + group * rows, :] = first.astype(BF16).astype(F32)

    sym = orb_sym_ref[...].reshape(1, n_orb)
    parity = jnp.bitwise_xor(column(sym, n_orb), jnp.concatenate([sym, sym], axis=1))
    for m in range(rows):
        part = first_ref[pl.ds(m, n_bas, stride=rows), :].astype(BF16)
        full = dot(orb_t, part, NN)
        block_ref[m * n_orb : (m + 1) * n_orb, :] = jnp.where(parity == pair_sym_ref[m], full, 0.0)
    low = lax.broadcasted_iota(jnp.int32, (rows, LANES), 1) < n_orb
    for h in range(n_orb * n_orb // WIDE):
        each = [block_ref[pl.ds(h * 4 + i, rows, stride=n_orb), :] for i in range(4)]
        left = jnp.where(low, each[0], each[1])
        right = jnp.where(low, each[2], each[3])
        table_ref[h * rows : (h + 1) * rows, :] = jnp.concatenate([left, right], axis=1).astype(BF16)


def couple(strings, own, win, rep, table_ref, g_ref, w_ref):
    win_target_ref, win_pair_ref, win_flip_ref = win
    rep_target_ref, rep_pair_ref, rep_flip_ref = rep
    groups = table_ref.shape[0] // 16
    rows = 16
    n_all = g_ref.shape[1]
    n_rep = rep_pair_ref.shape[1]
    n_win = win_pair_ref.shape[1]
    table = table_ref[...]
    inner = lax.broadcasted_iota(jnp.int32, (WIDE, n_rep), 0)
    m_own = lax.broadcasted_iota(jnp.int32, (rows, n_win), 0) + own * rows
    wide = []
    for a in strings:
        pair = rep_pair_ref[pl.ds(a, 1), :]
        spot = jnp.bitwise_and(pair, WIDE - 1)
        hit = jnp.where(inner == spot, 1.0, 0.0).astype(BF16)
        wide.append(dot(table, hit, NN))
    chosen, picks = [], []
    for a, y in zip(strings, wide):
        row = pl.ds(a, 1)
        group = jnp.broadcast_to(jnp.right_shift(rep_pair_ref[row, :], WIDE.bit_length() - 1), (rows, n_rep))
        total = y[:rows]
        for h in range(1, groups):
            total = jnp.where(group == h, y[h * rows : (h + 1) * rows], total)
        sign = (1 - 2 * rep_flip_ref[row, :]).astype(F32)
        chosen.append((total * sign).astype(BF16))
        w_sign = (1 - 2 * win_flip_ref[row, :]).astype(F32)
        picks.append(jnp.where(m_own == win_pair_ref[row, :], w_sign, 0.0).astype(BF16))

    def strings_tile(k):
        base = k * WIDE
        t = inner + base
        s = lax.broadcasted_iota(jnp.int32, (WIDE, n_win), 0) + base
        cols = pl.ds(pl.multiple_of(base, WIDE), WIDE)
        for u, a in enumerate(strings):
            row = pl.ds(a, 1)
            store = pl.ds(pl.multiple_of(a * rows, rows), rows)
            hit = jnp.where(t == rep_target_ref[row, :], 1.0, 0.0).astype(BF16)
            reach = jnp.where(s == win_target_ref[row, :], 1.0, 0.0).astype(BF16)
            g_ref[store, cols] = dot(chosen[u], hit, NT)
            w_ref[store, cols] = dot(picks[u], reach, NT)

    for_each(n_all // WIDE, strings_tile)


def kernel(
    n_sig, n_xf,
    coef_hbm, sym_alpha_hbm, sym_beta_hbm,
    win_target_hbm, win_pair_hbm, win_flip_hbm,
    rep_target_hbm, rep_pair_hbm, rep_flip_hbm,
    half_hbm, orb_hbm, orb_sym_hbm, pair_sym_ref,
    out_ref,
    coef_ref, sym_alpha_ref, sym_beta_ref,
    win_target_ref, win_pair_ref, win_flip_ref,
    rep_target_ref, rep_pair_ref, rep_flip_ref,
    half_ref, orb_ref, orb_sym_ref,
    first_ref, block_ref, table_ref, g_ref, w_ref,
    c_ref, q_ref, q_in, p_ref, p_in, h_ref,
    c_send, c_recv, q_send, q_recv, p_send, p_recv, h_send, h_recv, load_sem,
):
    me = lax.axis_index("sig")
    own = lax.axis_index("xf")
    own_rows, n_beta = coef_ref.shape
    n_all = own_rows * n_sig
    width = n_all // n_xf

    pairs = (
        (half_hbm, half_ref), (orb_hbm, orb_ref), (orb_sym_hbm, orb_sym_ref),
        (coef_hbm, coef_ref), (sym_alpha_hbm, sym_alpha_ref), (sym_beta_hbm, sym_beta_ref),
        (rep_pair_hbm, rep_pair_ref), (rep_target_hbm, rep_target_ref), (rep_flip_hbm, rep_flip_ref),
        (win_target_hbm, win_target_ref), (win_pair_hbm, win_pair_ref), (win_flip_hbm, win_flip_ref),
    )
    loads = [pltpu.make_async_copy(src, dst, load_sem.at[k]) for k, (src, dst) in enumerate(pairs)]
    for load in loads:
        load.start()

    barrier = pltpu.get_barrier_semaphore()

    def greet_sig(k):
        pl.semaphore_signal(barrier, inc=1, device_id=(lax.rem(me + k, n_sig), own), device_id_type=MESH)

    def greet_xf(k):
        pl.semaphore_signal(barrier, inc=1, device_id=(me, lax.rem(own + k, n_xf)), device_id_type=MESH)

    for k in range(1, n_sig):
        greet_sig(k)
    for k in range(1, n_xf):
        greet_xf(k)

    for load in loads[:6]:
        load.wait()
    sym_alpha = column(sym_alpha_ref[...].reshape(1, own_rows), own_rows)
    sym_beta = sym_beta_ref[...].reshape(1, n_beta)
    allowed = jnp.bitwise_xor(sym_alpha, sym_beta) == 0
    c_ref[me] = jnp.where(allowed, coef_ref[...].astype(F32), 0.0).astype(BF16)

    transform(half_ref, orb_ref, orb_sym_ref, pair_sym_ref, first_ref, block_ref, table_ref)


    def c_copy(k):
        return pltpu.make_async_remote_copy(
            src_ref=c_ref.at[me], dst_ref=c_ref.at[me], send_sem=c_send.at[k], recv_sem=c_recv.at[k],
            device_id=(lax.rem(me + k, n_sig), own), device_id_type=MESH)

    def c_arrival(k):
        slot = lax.rem(me + n_sig - k, n_sig)
        return pltpu.make_async_remote_copy(
            src_ref=c_ref.at[slot], dst_ref=c_ref.at[slot], send_sem=c_send.at[k], recv_sem=c_recv.at[k],
            device_id=(lax.rem(me + k, n_sig), own), device_id_type=MESH)

    def loop(low, high, step):
        lax.fori_loop(low, high, lambda k, _: (step(k), 0)[1], 0)

    for load in loads[6:]:
        load.wait()
    win = (win_target_ref, win_pair_ref, win_flip_ref)
    rep = (rep_target_ref, rep_pair_ref, rep_flip_ref)
    pl.semaphore_wait(barrier, n_sig + n_xf - 2)
    loop(1, n_sig, lambda k: c_copy(k).start())
    step = 4
    loop(0, own_rows // step, lambda a: couple(
        [a * step + u for u in range(step)], own, win, rep, table_ref, g_ref, w_ref))


    depth = g_ref.shape[0]
    tile = 256

    def q_tile(t, x):
        cols = pl.ds(pl.multiple_of(t * tile, tile), tile)
        lanes = pl.ds(pl.multiple_of(x * width, width), width)
        if depth == tile:
            high, low = split(g_ref[:, cols])
            w = w_ref[:, lanes].astype(BF16)
            total = dot(high, w, TN) + dot(low, w, TN)
        else:
            def part(k, total):
                ks = pl.ds(pl.multiple_of(k * tile, tile), tile)
                high, low = split(g_ref[ks, cols])
                w = w_ref[ks, lanes].astype(BF16)
                return total + dot(high, w, TN) + dot(low, w, TN)
            total = lax.fori_loop(0, depth // tile, part, jnp.zeros((tile, width), F32))
        q_ref[x, cols, :] = total

    for_each(n_xf, lambda x: for_each(n_all // tile, lambda t: q_tile(t, x)))

    def q_copy(k):
        there = lax.rem(own + k, n_xf)
        return pltpu.make_async_remote_copy(
            src_ref=q_ref.at[there], dst_ref=q_in.at[k - 1], send_sem=q_send.at[k - 1], recv_sem=q_recv.at[k - 1],
            device_id=(me, there), device_id_type=MESH)

    for k in range(1, n_xf):
        q_copy(k).start()
    for k in range(1, n_xf):
        q_copy(k).wait_recv()

    def p_block(t):
        rows = pl.ds(pl.multiple_of(t * tile, tile), tile)
        total = q_ref[own, rows, :]
        for k in range(n_xf - 1):
            total = total + q_in[k, rows, :]
        per = tile // own_rows
        p_ref[pl.ds(t * per, per)] = total.astype(BF16).reshape(per, own_rows, width)

    for_each(n_all // tile, p_block)

    def p_copy(k):
        there = lax.rem(me + k, n_sig)
        return pltpu.make_async_remote_copy(
            src_ref=p_ref.at[there], dst_ref=p_in.at[k], send_sem=p_send.at[k], recv_sem=p_recv.at[k],
            device_id=(there, own), device_id_type=MESH)

    loop(1, n_sig, lambda k: p_copy(k).start())
    p_in[0] = p_ref[me]
    loop(1, n_sig, lambda k: p_copy(k).wait_recv())
    h_ref[own] = jnp.sum(p_in[...].astype(F32), axis=0)

    def h_copy(k):
        return pltpu.make_async_remote_copy(
            src_ref=h_ref.at[own], dst_ref=h_ref.at[own], send_sem=h_send.at[k - 1], recv_sem=h_recv.at[k - 1],
            device_id=(me, lax.rem(own + k, n_xf)), device_id_type=MESH)

    def h_arrival(k):
        slot = lax.rem(own + n_xf - k, n_xf)
        return pltpu.make_async_remote_copy(
            src_ref=h_ref.at[slot], dst_ref=h_ref.at[slot], send_sem=h_send.at[k - 1], recv_sem=h_recv.at[k - 1],
            device_id=(me, lax.rem(own + k, n_xf)), device_id_type=MESH)

    for k in range(1, n_xf):
        h_copy(k).start()
    loop(1, n_sig, lambda k: c_arrival(k).wait_recv())
    for k in range(1, n_xf):
        h_arrival(k).wait_recv()
    high, low = split(jnp.concatenate([h_ref[x] for x in range(n_xf)], axis=1))
    c_all = c_ref[...].reshape(n_all, n_beta)
    total = dot(high, c_all, NN) + dot(low, c_all, NN)
    out_ref[...] = jnp.where(allowed, total, 0.0)

    loop(1, n_sig, lambda k: c_copy(k).wait_send())
    loop(1, n_sig, lambda k: p_copy(k).wait_send())
    for k in range(1, n_xf):
        q_copy(k).wait_send()
        h_copy(k).wait_send()


def body(n_sig, n_xf, *args):
    coef, half_ints, orbitals = args[0], args[9], args[10]
    own_rows, n_beta = coef.shape
    rows = half_ints.shape[0]
    n_bas, n_orb = orbitals.shape
    args = args[:10] + (orbitals.T,) + args[11:]
    n_all = own_rows * n_sig
    width = n_all // n_xf
    groups = n_orb * n_orb // WIDE
    vmem = pl.BlockSpec(memory_space=pltpu.VMEM)
    hbm = pl.BlockSpec(memory_space=pltpu.HBM)
    smem = pl.BlockSpec(memory_space=pltpu.SMEM)
    dma = pltpu.SemaphoreType.DMA
    return pl.pallas_call(
        functools.partial(kernel, n_sig, n_xf),
        out_shape=jax.ShapeDtypeStruct((own_rows, n_beta), F32),
        in_specs=[hbm] * 12 + [smem],
        out_specs=vmem,
        scratch_shapes=[pltpu.VMEM(arg.shape, arg.dtype) for arg in args[:12]] + [
            pltpu.VMEM((n_bas * rows, LANES), F32),
            pltpu.VMEM((rows * n_orb, LANES), F32),
            pltpu.VMEM((rows * groups, WIDE), BF16),
            pltpu.VMEM((own_rows * rows, n_all), F32),
            pltpu.VMEM((own_rows * rows, n_all), F32),
            pltpu.VMEM((n_sig, own_rows, n_beta), BF16),
            pltpu.VMEM((n_xf, n_all, width), F32),
            pltpu.VMEM((n_xf - 1, n_all, width), F32),
            pltpu.VMEM((n_sig, own_rows, width), BF16),
            pltpu.VMEM((n_sig, own_rows, width), BF16),
            pltpu.VMEM((n_xf, own_rows, width), F32),
            dma((n_sig,)), dma((n_sig,)),
            dma((n_xf - 1,)), dma((n_xf - 1,)),
            dma((n_sig,)), dma((n_sig,)),
            dma((n_xf - 1,)), dma((n_xf - 1,)),
            dma((12,)),
        ],
        compiler_params=pltpu.CompilerParams(
            collective_id=0, has_side_effects=True, vmem_limit_bytes=60 * 1024 * 1024
        ),
    )(*args)


def solution(mesh):
    in_specs = (
        P("sig", "xf"), P("sig"), P("xf"),
        P("sig", None), P("sig", None), P("sig", None),
        P("sig", None), P("sig", None), P("sig", None),
        P("xf", None), P(), P(), P("xf"),
    )
    step = functools.partial(body, mesh.shape["sig"], mesh.shape["xf"])
    return jax.shard_map(step, mesh=mesh, in_specs=in_specs, out_specs=P("sig", "xf"), check_vma=False)
```

```python
import functools

import jax
import jax.numpy as jnp
from jax import lax
from jax.experimental import pallas as pl
from jax.experimental.pallas import tpu as pltpu
from jax.sharding import PartitionSpec as P

MESH = pl.DeviceIdType.MESH
NT = (((1,), (1,)), ((), ()))
TN = (((0,), (0,)), ((), ()))
NN = (((1,), (0,)), ((), ()))
F32 = jnp.float32
BF16 = jnp.bfloat16
LANES = 128
WIDE = 256


def dot(x, y, dims):
    return lax.dot_general(x, y, dims, preferred_element_type=F32)


def split(x):
    high = x.astype(BF16)
    return high, (x - high.astype(F32)).astype(BF16)


def for_each(count, step):
    if count <= 2:
        for index in range(count):
            step(index)
    else:
        lax.fori_loop(0, count, lambda index, _: (step(index), 0)[1], 0)


def column(row, count):
    n = row.shape[1]
    mine = lax.broadcasted_iota(jnp.int32, (count, n), 0)
    other = lax.broadcasted_iota(jnp.int32, (count, n), 1)
    return jnp.sum(jnp.where(mine == other, row, 0), axis=1, keepdims=True)


def transform(half_ref, orb_ref, orb_sym_ref, pair_sym_ref, first_ref, block_ref, table_ref):
    rows = half_ref.shape[0]
    n_orb, n_bas = orb_ref.shape
    orb_t = orb_ref[...]
    twice = jnp.concatenate([orb_t, orb_t], axis=0)
    group = 16

    for c in range(n_bas // group):
        base = c * group * n_bas
        parts = [half_ref[:, base + k * n_bas : base + (k + 1) * n_bas] for k in range(group)]
        first = dot(jnp.concatenate(parts, axis=0), twice, NT)
        start = c * (group * rows)
        first_ref[start : start + group * rows, :] = first.astype(BF16).astype(F32)

    sym = orb_sym_ref[...].reshape(1, n_orb)
    parity = jnp.bitwise_xor(column(sym, n_orb), jnp.concatenate([sym, sym], axis=1))
    for m in range(rows):
        part = first_ref[pl.ds(m, n_bas, stride=rows), :].astype(BF16)
        full = dot(orb_t, part, NN)
        block_ref[m * n_orb : (m + 1) * n_orb, :] = jnp.where(parity == pair_sym_ref[m], full, 0.0)
    low = lax.broadcasted_iota(jnp.int32, (rows, LANES), 1) < n_orb
    for h in range(n_orb * n_orb // WIDE):
        each = [block_ref[pl.ds(h * 4 + i, rows, stride=n_orb), :] for i in range(4)]
        left = jnp.where(low, each[0], each[1])
        right = jnp.where(low, each[2], each[3])
        table_ref[h * rows : (h + 1) * rows, :] = jnp.concatenate([left, right], axis=1).astype(BF16)


def couple(strings, own, win, rep, table_ref, g_ref, w_ref):
    win_target_ref, win_pair_ref, win_flip_ref = win
    rep_target_ref, rep_pair_ref, rep_flip_ref = rep
    groups = table_ref.shape[0] // 16
    rows = 16
    n_all = g_ref.shape[1]
    n_rep = rep_pair_ref.shape[1]
    n_win = win_pair_ref.shape[1]
    table = table_ref[...]
    inner = lax.broadcasted_iota(jnp.int32, (WIDE, n_rep), 0)
    m_own = lax.broadcasted_iota(jnp.int32, (rows, n_win), 0) + own * rows
    wide = []
    for a in strings:
        pair = rep_pair_ref[pl.ds(a, 1), :]
        spot = jnp.bitwise_and(pair, WIDE - 1)
        hit = jnp.where(inner == spot, 1.0, 0.0).astype(BF16)
        wide.append(dot(table, hit, NN))
    chosen, picks = [], []
    for a, y in zip(strings, wide):
        row = pl.ds(a, 1)
        group = jnp.broadcast_to(jnp.right_shift(rep_pair_ref[row, :], WIDE.bit_length() - 1), (rows, n_rep))
        total = y[:rows]
        for h in range(1, groups):
            total = jnp.where(group == h, y[h * rows : (h + 1) * rows], total)
        sign = (1 - 2 * rep_flip_ref[row, :]).astype(F32)
        chosen.append((total * sign).astype(BF16))
        w_sign = (1 - 2 * win_flip_ref[row, :]).astype(F32)
        picks.append(jnp.where(m_own == win_pair_ref[row, :], w_sign, 0.0).astype(BF16))

    def strings_tile(k):
        base = k * WIDE
        t = inner + base
        s = lax.broadcasted_iota(jnp.int32, (WIDE, n_win), 0) + base
        cols = pl.ds(pl.multiple_of(base, WIDE), WIDE)
        for u, a in enumerate(strings):
            row = pl.ds(a, 1)
            store = pl.ds(pl.multiple_of(a * rows, rows), rows)
            hit = jnp.where(t == rep_target_ref[row, :], 1.0, 0.0).astype(BF16)
            reach = jnp.where(s == win_target_ref[row, :], 1.0, 0.0).astype(BF16)
            g_ref[store, cols] = dot(chosen[u], hit, NT)
            w_ref[store, cols] = dot(picks[u], reach, NT)

    for_each(n_all // WIDE, strings_tile)


def kernel(
    n_sig, n_xf,
    coef_hbm, sym_alpha_hbm, sym_beta_hbm,
    win_target_hbm, win_pair_hbm, win_flip_hbm,
    rep_target_hbm, rep_pair_hbm, rep_flip_hbm,
    half_hbm, orb_hbm, orb_sym_hbm, pair_sym_ref,
    out_ref,
    coef_ref, sym_alpha_ref, sym_beta_ref,
    win_target_ref, win_pair_ref, win_flip_ref,
    rep_target_ref, rep_pair_ref, rep_flip_ref,
    half_ref, orb_ref, orb_sym_ref,
    first_ref, block_ref, table_ref, g_ref, w_ref,
    c_ref, q_ref, q_in, p_ref, p_in, h_ref,
    c_send, c_recv, q_send, q_recv, p_send, p_recv, h_send, h_recv, load_sem,
):
    me = lax.axis_index("sig")
    own = lax.axis_index("xf")
    own_rows, n_beta = coef_ref.shape
    n_all = own_rows * n_sig
    width = n_all // n_xf

    pairs = (
        (half_hbm, half_ref), (orb_hbm, orb_ref), (orb_sym_hbm, orb_sym_ref),
        (coef_hbm, coef_ref), (sym_alpha_hbm, sym_alpha_ref), (sym_beta_hbm, sym_beta_ref),
        (rep_pair_hbm, rep_pair_ref), (rep_target_hbm, rep_target_ref), (rep_flip_hbm, rep_flip_ref),
        (win_target_hbm, win_target_ref), (win_pair_hbm, win_pair_ref), (win_flip_hbm, win_flip_ref),
    )
    loads = [pltpu.make_async_copy(src, dst, load_sem.at[k]) for k, (src, dst) in enumerate(pairs)]
    for load in loads:
        load.start()

    barrier = pltpu.get_barrier_semaphore()

    def greet_sig(k):
        pl.semaphore_signal(barrier, inc=1, device_id=(lax.rem(me + k, n_sig), own), device_id_type=MESH)

    def greet_xf(k):
        pl.semaphore_signal(barrier, inc=1, device_id=(me, lax.rem(own + k, n_xf)), device_id_type=MESH)

    for k in range(1, n_sig):
        greet_sig(k)
    for k in range(1, n_xf):
        greet_xf(k)

    for load in loads[:6]:
        load.wait()
    sym_alpha = column(sym_alpha_ref[...].reshape(1, own_rows), own_rows)
    sym_beta = sym_beta_ref[...].reshape(1, n_beta)
    allowed = jnp.bitwise_xor(sym_alpha, sym_beta) == 0
    c_ref[me] = jnp.where(allowed, coef_ref[...].astype(F32), 0.0).astype(BF16)

    transform(half_ref, orb_ref, orb_sym_ref, pair_sym_ref, first_ref, block_ref, table_ref)


    def c_copy(k):
        return pltpu.make_async_remote_copy(
            src_ref=c_ref.at[me], dst_ref=c_ref.at[me], send_sem=c_send.at[k], recv_sem=c_recv.at[k],
            device_id=(lax.rem(me + k, n_sig), own), device_id_type=MESH)

    def c_arrival(k):
        slot = lax.rem(me + n_sig - k, n_sig)
        return pltpu.make_async_remote_copy(
            src_ref=c_ref.at[slot], dst_ref=c_ref.at[slot], send_sem=c_send.at[k], recv_sem=c_recv.at[k],
            device_id=(lax.rem(me + k, n_sig), own), device_id_type=MESH)

    def loop(low, high, step):
        lax.fori_loop(low, high, lambda k, _: (step(k), 0)[1], 0)

    def each(low, high, step):
        for k in range(low, high):
            step(k)

    for load in loads[6:]:
        load.wait()
    win = (win_target_ref, win_pair_ref, win_flip_ref)
    rep = (rep_target_ref, rep_pair_ref, rep_flip_ref)
    pl.semaphore_wait(barrier, n_sig + n_xf - 2)
    each(1, n_sig, lambda k: c_copy(k).start())
    step = 4
    loop(0, own_rows // step, lambda a: couple(
        [a * step + u for u in range(step)], own, win, rep, table_ref, g_ref, w_ref))


    depth = g_ref.shape[0]
    tile = 256

    def q_tile(t, x):
        cols = pl.ds(pl.multiple_of(t * tile, tile), tile)
        lanes = pl.ds(pl.multiple_of(x * width, width), width)
        if depth == tile:
            high, low = split(g_ref[:, cols])
            w = w_ref[:, lanes].astype(BF16)
            total = dot(high, w, TN) + dot(low, w, TN)
        else:
            def part(k, total):
                ks = pl.ds(pl.multiple_of(k * tile, tile), tile)
                high, low = split(g_ref[ks, cols])
                w = w_ref[ks, lanes].astype(BF16)
                return total + dot(high, w, TN) + dot(low, w, TN)
            total = lax.fori_loop(0, depth // tile, part, jnp.zeros((tile, width), F32))
        q_ref[x, cols, :] = total

    if depth == tile and n_all == tile:
        high, low = split(g_ref[...])
        w = w_ref[...].astype(BF16)
        total = dot(high, w, TN) + dot(low, w, TN)
        for x in range(n_xf):
            q_ref[x] = total[:, x * width : (x + 1) * width]
    else:
        for_each(n_xf, lambda x: for_each(n_all // tile, lambda t: q_tile(t, x)))

    def q_copy(k):
        there = lax.rem(own + k, n_xf)
        return pltpu.make_async_remote_copy(
            src_ref=q_ref.at[there], dst_ref=q_in.at[k - 1], send_sem=q_send.at[k - 1], recv_sem=q_recv.at[k - 1],
            device_id=(me, there), device_id_type=MESH)

    for k in range(1, n_xf):
        q_copy(k).start()
    for k in range(1, n_xf):
        q_copy(k).wait_recv()

    def p_block(t):
        rows = pl.ds(pl.multiple_of(t * tile, tile), tile)
        total = q_ref[own, rows, :]
        for k in range(n_xf - 1):
            total = total + q_in[k, rows, :]
        per = tile // own_rows
        p_ref[pl.ds(t * per, per)] = total.astype(BF16).reshape(per, own_rows, width)

    for_each(n_all // tile, p_block)

    def p_copy(k):
        there = lax.rem(me + k, n_sig)
        return pltpu.make_async_remote_copy(
            src_ref=p_ref.at[there], dst_ref=p_in.at[k], send_sem=p_send.at[k], recv_sem=p_recv.at[k],
            device_id=(there, own), device_id_type=MESH)

    each(1, n_sig, lambda k: p_copy(k).start())
    p_in[0] = p_ref[me]
    each(1, n_sig, lambda k: p_copy(k).wait_recv())
    h_ref[own] = jnp.sum(p_in[...].astype(F32), axis=0)

    def h_copy(k):
        return pltpu.make_async_remote_copy(
            src_ref=h_ref.at[own], dst_ref=h_ref.at[own], send_sem=h_send.at[k - 1], recv_sem=h_recv.at[k - 1],
            device_id=(me, lax.rem(own + k, n_xf)), device_id_type=MESH)

    def h_arrival(k):
        slot = lax.rem(own + n_xf - k, n_xf)
        return pltpu.make_async_remote_copy(
            src_ref=h_ref.at[slot], dst_ref=h_ref.at[slot], send_sem=h_send.at[k - 1], recv_sem=h_recv.at[k - 1],
            device_id=(me, lax.rem(own + k, n_xf)), device_id_type=MESH)

    for k in range(1, n_xf):
        h_copy(k).start()
    each(1, n_sig, lambda k: c_arrival(k).wait_recv())
    for k in range(1, n_xf):
        h_arrival(k).wait_recv()
    high, low = split(jnp.concatenate([h_ref[x] for x in range(n_xf)], axis=1))
    c_all = c_ref[...].reshape(n_all, n_beta)
    total = dot(high, c_all, NN) + dot(low, c_all, NN)
    out_ref[...] = jnp.where(allowed, total, 0.0)

    each(1, n_sig, lambda k: c_copy(k).wait_send())
    each(1, n_sig, lambda k: p_copy(k).wait_send())
    for k in range(1, n_xf):
        q_copy(k).wait_send()
        h_copy(k).wait_send()


def body(n_sig, n_xf, *args):
    coef, half_ints, orbitals = args[0], args[9], args[10]
    own_rows, n_beta = coef.shape
    rows = half_ints.shape[0]
    n_bas, n_orb = orbitals.shape
    args = args[:10] + (orbitals.T,) + args[11:]
    n_all = own_rows * n_sig
    width = n_all // n_xf
    groups = n_orb * n_orb // WIDE
    vmem = pl.BlockSpec(memory_space=pltpu.VMEM)
    hbm = pl.BlockSpec(memory_space=pltpu.HBM)
    smem = pl.BlockSpec(memory_space=pltpu.SMEM)
    dma = pltpu.SemaphoreType.DMA
    return pl.pallas_call(
        functools.partial(kernel, n_sig, n_xf),
        out_shape=jax.ShapeDtypeStruct((own_rows, n_beta), F32),
        in_specs=[hbm] * 12 + [smem],
        out_specs=vmem,
        scratch_shapes=[pltpu.VMEM(arg.shape, arg.dtype) for arg in args[:12]] + [
            pltpu.VMEM((n_bas * rows, LANES), F32),
            pltpu.VMEM((rows * n_orb, LANES), F32),
            pltpu.VMEM((rows * groups, WIDE), BF16),
            pltpu.VMEM((own_rows * rows, n_all), F32),
            pltpu.VMEM((own_rows * rows, n_all), F32),
            pltpu.VMEM((n_sig, own_rows, n_beta), BF16),
            pltpu.VMEM((n_xf, n_all, width), F32),
            pltpu.VMEM((n_xf - 1, n_all, width), F32),
            pltpu.VMEM((n_sig, own_rows, width), BF16),
            pltpu.VMEM((n_sig, own_rows, width), BF16),
            pltpu.VMEM((n_xf, own_rows, width), F32),
            dma((n_sig,)), dma((n_sig,)),
            dma((n_xf - 1,)), dma((n_xf - 1,)),
            dma((n_sig,)), dma((n_sig,)),
            dma((n_xf - 1,)), dma((n_xf - 1,)),
            dma((12,)),
        ],
        compiler_params=pltpu.CompilerParams(
            collective_id=0, has_side_effects=True, vmem_limit_bytes=60 * 1024 * 1024
        ),
    )(*args)


def solution(mesh):
    in_specs = (
        P("sig", "xf"), P("sig"), P("xf"),
        P("sig", None), P("sig", None), P("sig", None),
        P("sig", None), P("sig", None), P("sig", None),
        P("xf", None), P(), P(), P("xf"),
    )
    step = functools.partial(body, mesh.shape["sig"], mesh.shape["xf"])
    return jax.shard_map(step, mesh=mesh, in_specs=in_specs, out_specs=P("sig", "xf"), check_vma=False)
```
